768 devices in a mesh: grp: 64 (over y, x, core), loc: 12 (over z).
Axes of the slice: x: 4, y: 8, z: 12, core: 2. Of those that a mesh axis runs over, the one named last changes fastest.
Arguments:
- grad_rows: float32 [786432, 128], P(('grp', 'loc')), may hold values from -24 to 24
- row_owner: int32 [786432, 1], P(('grp', 'loc')), may hold values from 0 to 767; in each aligned block of 1024 rows (0 to 1023, 1024 to 2047, ...) at most 3 rows name the same one
- row_slot: int32 [786432], P(('grp', 'loc')), may hold values from 0 to 1023
- weights: float32 [786432, 128], P(('grp', 'loc')), may hold values from -6 to 6
- first_moment: float32 [786432, 128], P(('grp', 'loc')), may hold values from -6 to 6
- second_moment: float32 [786432, 128], P(('grp', 'loc')), may hold values from 1 to 10
Outputs:
- new_weights: float32 [786432, 128], P(('grp', 'loc'))
- new_first: float32 [786432, 128], P(('grp', 'loc'))
- new_second: float32 [786432, 128], P(('grp', 'loc'))
The draws below stay inside these ranges and needn't reach their ends.
Inputs may be any that keep to these rules, and one draw needn't show every extreme that they name: `row_owner`: among the rows of one device no owner is named by more than 3 rows, a bound that some block reaches.
All inputs are finite; a program needn't handle non-finite values.
Results may differ from the reference program's by a relative error of at most 0.00005.
Values sent between devices are 32-bit elements; how exact they have to be, the bound alone decides.
A program may use at most 32 MiB of HBM per device.

```python
import math
import jax
import jax.numpy as jnp
import numpy as np

WIDTH = 128
ROWS_DEV = 1024
SHARD_ROWS = 1024
STEP = 1000
CAP = 3
TOTAL_ROWS = 786432
TABLE_ROWS = 786432
DEVICES = 768


def set_ends(array, own_key, smallest, top_value):
    longest = array.shape.index(max(array.shape))
    spots = []
    for shift in (0, 1):
        where = [jax.random.randint(jax.random.fold_in(own_key, axis), (), 0, length) for axis, length in enumerate(array.shape)]
        where[longest] = (where[longest] + shift) % array.shape[longest]
        spots.append(tuple(where))
    return array.at[spots[0]].set(smallest).at[spots[1]].set(top_value)


def level_of(stream_key, shape, pieces, low, top_value):
    factor_of, own = 1.0, jax.random.fold_in(stream_key, 6)
    for dim, blocks in pieces:
        steps = jnp.exp(jax.random.uniform(jax.random.fold_in(own, dim), (blocks,), jnp.float32, low / len(pieces), top_value / len(pieces)))
        factor_of = factor_of * jnp.repeat(steps, shape[dim] // blocks).reshape([-1 if axis == dim else 1 for axis in range(len(shape))])
    return factor_of


def routed_block(key, own, number, rows, amount, top, reach, lean):
    sequence = jax.random.permutation(key, amount)
    heavy_load, ordinary = portions_of(amount, rows * top, reach, lean, True), portions_of(amount, rows * top, reach, lean, False)
    places = jnp.arange(amount)

    def named(tallies, turn):
        used = int((tallies > 0).sum())
        fixed = max(1, used // 4)
        moved = fixed + (places - fixed + turn * (used - fixed)) % max(1, amount - fixed)
        return jnp.zeros((amount,), jnp.int32).at[sequence[jnp.where(places < fixed, places, moved)]].set(jnp.asarray(tallies, jnp.int32))

    tallies = jnp.where(number % 4 == 0, named(heavy_load, number // 4), named(ordinary, number - number // 4 - 1))
    mixed = jax.random.permutation(jax.random.fold_in(own, 3), amount)
    giver, sink = mixed[0:amount // 2 * 2:2], mixed[1:amount // 2 * 2:2]
    room = jnp.minimum(tallies[giver] - 1, reach - tallies[sink]) // 2
    room = jnp.where((giver == sequence[0]) | (sink == sequence[0]) | (tallies[sink] == 0), 0, jnp.maximum(room, 0))
    moved = jax.random.randint(jax.random.fold_in(own, 4), (amount // 2,), 0, 1 << 20) % (room + 1)
    tallies = tallies.at[giver].add(-moved).at[sink].add(moved)
    members = jnp.searchsorted(jnp.cumsum(tallies), jnp.arange(rows * top), side="right").astype(jnp.int32)
    table = members.reshape(top, rows).T
    table = table[jax.random.permutation(jax.random.fold_in(own, 1), rows)]
    turn = jax.random.randint(jax.random.fold_in(own, 2), (rows, 1), 0, top)
    return jnp.take_along_axis(table, (jnp.arange(top)[None, :] + turn) % top, axis=1)


def portions_of(count, total, reach, lean, full):
    weights = [(1 << 20) // math.isqrt(standing ** lean) + 1 for standing in range(1, count + 1)]
    largest = reach if full else min(reach, max(-(-total // count), total * weights[0] // sum(weights)))
    least = 1 if total - largest >= count - 1 else 0
    given, rest = [largest] + [least] * (count - 1), total - largest - least * (count - 1)
    while rest > 0:
        movable = [i for i in range(1, count) if given[i] < largest] or [i for i in range(1, count) if given[i] < reach]
        whole, remaining = sum([weights[i] for i in movable]), rest
        for i in movable:
            more = min(reach - given[i], max(1, remaining * weights[i] // whole), rest)
            given[i] = given[i] + more
            rest = rest - more
    return np.array(given)


def noise(stream_key, dims, width, limit, shards=(), dtype=jnp.bfloat16):
    array = width * jax.random.normal(stream_key, dims, jnp.float32)
    if shards:
        array = array * level_of(stream_key, dims, shards, -0.22, 0.18)
    return jnp.clip(array, -limit, limit).astype(dtype)


def setup_inputs(seed: int = 0) -> dict:
    seeds = jax.random.split(jax.random.key(seed), 7)
    grad_rows = noise(seeds[0], (TOTAL_ROWS, WIDTH), 4.0, 24.0, ((0, 768),), jnp.float32)
    row_owner_keys = jax.random.split(jax.random.fold_in(seeds[1], 1), TOTAL_ROWS // ROWS_DEV)
    row_owner_turns = jax.random.permutation(jax.random.fold_in(seeds[1], 3), TOTAL_ROWS // ROWS_DEV)
    row_owner = jax.vmap(lambda own, number: routed_block(jax.random.fold_in(seeds[1], 2), own, number, ROWS_DEV, DEVICES, 1, CAP, 2))(row_owner_keys, row_owner_turns).reshape((TOTAL_ROWS, 1))
    row_slot = set_ends(jax.random.randint(seeds[2], (TOTAL_ROWS,), 0, SHARD_ROWS), jax.random.fold_in(seeds[2], 1), 0, SHARD_ROWS - 1).astype(jnp.int32)
    weights = noise(seeds[3], (TABLE_ROWS, WIDTH), 1.0, 6.0, ((0, 768),), jnp.float32)
    first_moment = noise(seeds[4], (TABLE_ROWS, WIDTH), 1.0, 6.0, ((0, 768),), jnp.float32)
    second_moment = jnp.clip(jnp.exp(math.log(10.0) - 2.3025851 * jax.random.uniform(seeds[5], (TABLE_ROWS, WIDTH), jnp.float32) ** level_of(seeds[5], (TABLE_ROWS, WIDTH), ((0, 768),), -0.2, 0.2)), 1.0, 10.0)
    return {"grad_rows": grad_rows, "row_owner": row_owner, "row_slot": row_slot, "weights": weights, "first_moment": first_moment, "second_moment": second_moment}


def reference(grad_rows, row_owner, row_slot, weights, first_moment, second_moment):
    target = (row_owner[:, 0] * SHARD_ROWS + row_slot).astype(jnp.int32)
    summed = jax.ops.segment_sum(grad_rows, target, num_segments=TABLE_ROWS)
    touched = jax.ops.segment_sum(jnp.ones_like(target), target, num_segments=TABLE_ROWS)
    active = (touched > 0)[:, None]
    first_next = 0.9 * first_moment + 0.1 * summed
    second_next = 0.99 * second_moment + 0.01 * summed * summed
    first_hat = first_next / (1.0 - 0.9 ** STEP)
    second_hat = second_next / (1.0 - 0.99 ** STEP)
    weights_next = weights - 0.5 * first_hat / (jnp.sqrt(second_hat) + 1e-08)
    new_first = jnp.where(active, first_next, first_moment)
    new_second = jnp.where(active, second_next, second_moment)
    new_weights = jnp.where(active, weights_next, weights)
    return (new_weights, new_first, new_second)
```

```python
import jax
import jax.numpy as jnp
from jax import lax
from jax.experimental import pallas as pl
from jax.experimental.pallas import tpu as pltpu
from jax.sharding import PartitionSpec as P

STEP = 1000
VMEM = 60 * 1024 * 1024
MESH = pl.DeviceIdType.MESH
F32, BF16, I32 = jnp.float32, jnp.bfloat16, jnp.int32

NY, NXC, NL, CAP = 8, 8, 12, 3
ROWS, WIDTH = 1024, 128
ZROWS = NXC * CAP
SROWS = 40
LANES = NXC * SROWS


def iota(shape, dim):
    return lax.broadcasted_iota(I32, shape, dim)


def onehot(mask):
    return jnp.where(mask, 1.0, 0.0).astype(BF16)


def split(value):
    high = value.astype(BF16)
    low = (value - high.astype(F32)).astype(BF16)
    return jnp.concatenate([high, low], axis=1)


def join(value):
    return value[:, :WIDTH] + value[:, WIDTH:]


def dot(a, b):
    return jnp.dot(a, b, preferred_element_type=F32)


def dot_t(a, b):
    return lax.dot_general(a, b, (((1,), (1,)), ((), ())), preferred_element_type=F32)


def y_distance(chunk):
    hops = (8 - chunk) // 2
    return hops if chunk % 2 else (8 - hops) % 8


def exchange(
    grad_hbm, owner_hbm, slot_hbm, weights_hbm, first_hbm, second_hbm, new_weights, new_first, new_second,
    grad, owner, slot, weights, first, second, parts, zsend, zrecv, zslot_send, zslot_recv, ssend, frecv, wslots, place, acc, count,
    zsem, zrsem, zssem, zsrsem, ssem, frsem, insem,
):
    load = pltpu.make_async_copy(grad_hbm, grad, insem.at[0])
    load.start()
    ids = [
        pltpu.make_async_copy(owner_hbm, owner, insem.at[4]),
        pltpu.make_async_copy(slot_hbm, slot, insem.at[5]),
    ]
    for copy in ids:
        copy.start()
    grp, loc = lax.axis_index("grp"), lax.axis_index("loc")
    my_y, my_xc = grp // NXC, lax.rem(grp, NXC)

    barrier = pltpu.get_barrier_semaphore()
    for step in range(1, NL):
        pl.semaphore_signal(
            barrier, inc=1, device_id=(grp, lax.rem(loc + step, NL)), device_id_type=MESH
        )

    @pl.loop(1, NY * NXC)
    def _(step):
        pl.semaphore_signal(
            barrier, inc=1, device_id=(lax.rem(grp + step, NY * NXC), loc), device_id_type=MESH
        )

    for copy in ids:
        copy.wait()
    own = owner[...]
    group = lax.shift_right_logical(own * 43691, 19)
    index = own - NL * group
    distance = jnp.bitwise_and(lax.shift_right_logical(group, 3) - my_y + NY, NY - 1)
    xc = jnp.bitwise_and(group, NXC - 1)
    hops = jnp.minimum(distance, NY - distance)
    chunk = jnp.maximum(0, 7 - 2 * hops + (distance > 4).astype(I32))

    def rows(tile):
        return jnp.concatenate([tile[b : b + 1, :] for b in range(8)], axis=1)

    own_f = own.astype(F32)
    own_row = rows(own_f)
    own_col = jnp.concatenate([own_f] * 16, axis=0).T
    earlier = iota((128, 128), 0) < iota((128, 128), 1)
    ranks = []
    for ib in range(8):
        mine = own_row[:, ib * 128 : (ib + 1) * 128]
        total = jnp.zeros((128, 128), F32)
        for jb in range(ib + 1):
            same = own_col[:, jb : jb + 1] == mine
            if jb == ib:
                same = jnp.logical_and(same, earlier)
            total = total + jnp.where(same, 1.0, 0.0)
        ranks.append(jnp.sum(total, axis=0, keepdims=True))
    rank = jnp.concatenate(ranks, axis=1).astype(I32)
    chunk_row, index_row, xc_row = rows(chunk), rows(index), rows(xc)
    code = chunk_row * (NL * ZROWS) + index_row * ZROWS + xc_row * CAP + rank

    slot_row = rows(slot[...]) + 1
    line = index_row * NY + chunk_row == iota((NL * NY, ROWS), 0)
    high = lax.shift_right_logical(slot_row, 5).astype(F32)
    low = jnp.bitwise_and(slot_row, 31).astype(F32)
    lines = jnp.concatenate([jnp.where(line, high, 0.0), jnp.where(line, low, 0.0)], axis=0)
    place_lane = onehot(rank * NXC + xc_row == iota((128, ROWS), 0))
    slots = dot_t(lines.astype(BF16), place_lane)
    slots = 32.0 * slots[: NL * NY] + slots[NL * NY :]
    zslot_send[...] = slots.reshape(NL, NY, 128)

    load.wait()
    parts[...] = split(grad[...])

    def z_compute(c):
        pick = onehot(code == iota((NL * ZROWS, ROWS), 0) + c * (NL * ZROWS))
        out = join(dot(pick, parts[...]))
        zsend[c] = out.reshape(NL, ZROWS, WIDTH)
        zrecv[c, loc] = zsend[c, loc]

    z_compute(0)
    zslot_recv[loc] = zslot_send[loc]
    pl.semaphore_wait(barrier, NL - 1 + NY * NXC - 1)

    z_order = (6, 5, 7, 4, 8, 3, 9, 2, 10, 1, 11)
    for step in z_order:
        to = lax.rem(loc + step, NL)
        pltpu.make_async_remote_copy(
            zslot_send.at[to], zslot_recv.at[loc], zssem, zsrsem,
            device_id=(grp, to), device_id_type=MESH,
        ).start()

    def z_send(c):
        for step in z_order:
            to = lax.rem(loc + step, NL)
            pltpu.make_async_remote_copy(
                zsend.at[c, to], zrecv.at[c, loc], zsem.at[c], zrsem.at[c],
                device_id=(grp, to), device_id_type=MESH,
            ).start()

    def wait(block, sem):
        pltpu.make_async_copy(block, block, sem).wait()

    z_send(0)
    for c in range(1, NY):
        z_compute(c)
        z_send(c)

    tables = [
        pltpu.make_async_copy(weights_hbm, weights, insem.at[1]),
        pltpu.make_async_copy(first_hbm, first, insem.at[2]),
        pltpu.make_async_copy(second_hbm, second, insem.at[3]),
    ]
    for table in tables:
        table.start()

    to_row, from_row = iota((LANES, NL * ZROWS), 0), iota((LANES, NL * ZROWS), 1)
    to_xc, to_rest = to_row // SROWS, to_row % SROWS
    wanted = (to_rest // CAP) * ZROWS + to_xc * CAP + to_rest % CAP
    place[...] = onehot(jnp.logical_and(wanted == from_row, to_rest < NL * CAP))
    acc[...] = jnp.zeros_like(acc)
    count[...] = jnp.zeros_like(count)

    wait(zslot_send.at[pl.ds(0, NL - 1)], zsrsem)
    got = jnp.concatenate([zslot_recv[...].reshape(NL * NY, 128), jnp.zeros((32, 128), F32)], axis=0).T
    high = jnp.floor(got * (1.0 / 32.0))
    low = got - 32.0 * high
    lane = iota((128, 384), 1) - my_xc * SROWS
    line = iota((128, 384), 0)
    for c in range(NY):
        total = jnp.zeros((NXC, 384), F32)
        for k in range(CAP):
            part = slice(k * NXC, (k + 1) * NXC)
            both = jnp.concatenate([high[part], low[part]], axis=0).astype(BF16)
            at = onehot(jnp.logical_and(lane == (line // NY) * CAP + k, line % NY == c))
            moved = dot(both, at)
            total = total + 32.0 * moved[:NXC] + moved[NXC:]
        wslots[c] = total

    def s_stage(c):
        wait(zsend.at[c, pl.ds(0, NL - 1)], zrsem.at[c])
        moved = join(dot(place[...], split(zrecv[c].reshape(NL * ZROWS, WIDTH))))
        ssend[c] = moved.reshape(NXC, SROWS, WIDTH)
        for x in range(NXC):
            for t in range(3):
                row = NL * CAP + t
                ssend[c, x, row : row + 1, :] = wslots[c, x : x + 1, t * 128 : (t + 1) * 128]
        away = y_distance(c)
        to_y = lax.rem(my_y + away, NY)
        for step in range(NXC):
            to = lax.rem(my_xc + step, NXC)
            if away == 0 and step == 0:
                frecv[c, my_xc] = ssend[c, my_xc]
                continue
            pltpu.make_async_remote_copy(
                ssend.at[c, to], frecv.at[c, my_xc], ssem.at[c], frsem.at[c],
                device_id=(to_y * NXC + to, loc), device_id_type=MESH,
            ).start()

    def f_stage(c):
        many = NXC - 1 if y_distance(c) == 0 else NXC
        wait(ssend.at[c, pl.ds(0, many)], frsem.at[c])
        got = frecv[c]
        line = jnp.sum(got[:, NL * CAP : NL * CAP + 3, :], axis=0)
        line = jnp.concatenate([line[t : t + 1, :] for t in range(3)], axis=1).astype(I32)
        data = split(got.reshape(LANES, WIDTH))

        @pl.loop(0, 4)
        def _(b):
            at = pl.ds(pl.multiple_of(b * 256, 256), 256)
            hit = jnp.where(line == iota((256, 384), 0) + (b * 256 + 1), 1.0, 0.0)
            acc[at, :] += dot(hit[:, :LANES].astype(BF16), data)
            count[at, :] += hit[:, :128] + hit[:, 128:256] + hit[:, 256:]

    s_stage(0)
    s_stage(1)
    for c in range(2, 7):
        s_stage(c)
        f_stage(c - 2)
    f_stage(5)
    s_stage(7)
    f_stage(6)
    for table in tables:
        table.wait()
    f_stage(7)

    for b in range(4):
        at = pl.ds(b * 256, 256)
        summed = join(acc[at, :])
        active = dot(count[at, :].astype(BF16), jnp.ones((128, WIDTH), BF16)) > 0.5
        old_first, old_second, old_weights = first[at, :], second[at, :], weights[at, :]
        first_next = 0.9 * old_first + 0.1 * summed
        second_next = 0.99 * old_second + 0.01 * summed * summed
        first_hat = first_next / (1.0 - 0.9**STEP)
        second_hat = second_next / (1.0 - 0.99**STEP)
        weights_next = old_weights - 0.5 * first_hat / (jnp.sqrt(second_hat) + 1e-08)
        new_first[at, :] = jnp.where(active, first_next, old_first)
        new_second[at, :] = jnp.where(active, second_next, old_second)
        new_weights[at, :] = jnp.where(active, weights_next, old_weights)

    wait(zslot_send.at[pl.ds(0, NL - 1)], zssem)
    for c in range(NY):
        wait(zsend.at[c, pl.ds(0, NL - 1)], zsem.at[c])
        many = NXC - 1 if y_distance(c) == 0 else NXC
        wait(ssend.at[c, pl.ds(0, many)], ssem.at[c])


def store(weights, first, second, weights_hbm, first_hbm, second_hbm, sems):
    pairs = ((weights, weights_hbm), (first, first_hbm), (second, second_hbm))
    copies = [pltpu.make_async_copy(a, b, sems.at[i]) for i, (a, b) in enumerate(pairs)]
    for copy in copies:
        copy.start()
    for copy in copies:
        copy.wait()


def on_device(grad_rows, row_owner, row_slot, weights, first_moment, second_moment):
    vmem = pl.BlockSpec(memory_space=pltpu.VMEM)
    dma = pltpu.SemaphoreType.DMA
    hbm = pl.BlockSpec(memory_space=pltpu.HBM)
    out = jax.ShapeDtypeStruct((ROWS, WIDTH), F32)
    results = pl.pallas_call(
        exchange,
        out_shape=(out, out, out),
        in_specs=[hbm] * 6,
        out_specs=(vmem, vmem, vmem),
        scratch_shapes=[
            pltpu.VMEM((ROWS, WIDTH), F32),
            pltpu.VMEM((8, 128), I32),
            pltpu.VMEM((8, 128), I32),
            pltpu.VMEM((ROWS, WIDTH), F32),
            pltpu.VMEM((ROWS, WIDTH), F32),
            pltpu.VMEM((ROWS, WIDTH), F32),
            pltpu.VMEM((ROWS, 2 * WIDTH), BF16),
            pltpu.VMEM((NY, NL, ZROWS, WIDTH), F32),
            pltpu.VMEM((NY, NL, ZROWS, WIDTH), F32),
            pltpu.VMEM((NL, NY, 128), F32),
            pltpu.VMEM((NL, NY, 128), F32),
            pltpu.VMEM((NY, NXC, SROWS, WIDTH), F32),
            pltpu.VMEM((NY, NXC, SROWS, WIDTH), F32),
            pltpu.VMEM((NY, NXC, 384), F32),
            pltpu.VMEM((LANES, NL * ZROWS), BF16),
            pltpu.VMEM((ROWS, 2 * WIDTH), F32),
            pltpu.VMEM((ROWS, 128), F32),
            dma((NY,)),
            dma((NY,)),
            dma,
            dma,
            dma((NY,)),
            dma((NY,)),
            dma((6,)),
        ],
        compiler_params=pltpu.CompilerParams(
            collective_id=0, has_side_effects=True, vmem_limit_bytes=VMEM
        ),
        name="exchange",
    )(
        grad_rows, row_owner.reshape(8, 128), row_slot.reshape(8, 128),
        weights, first_moment, second_moment,
    )
    return pl.pallas_call(
        store,
        out_shape=(out, out, out),
        in_specs=[vmem] * 3,
        out_specs=(hbm, hbm, hbm),
        scratch_shapes=[dma((3,))],
        compiler_params=pltpu.CompilerParams(vmem_limit_bytes=VMEM),
        name="store",
    )(*results)


def solution(mesh):
    placed = (
        P(("grp", "loc"), None),
        P(("grp", "loc"), None),
        P(("grp", "loc")),
        P(("grp", "loc"), None),
        P(("grp", "loc"), None),
        P(("grp", "loc"), None),
    )
    return jax.shard_map(
        on_device,
        mesh=mesh,
        in_specs=placed,
        out_specs=(P(("grp", "loc"), None), P(("grp", "loc"), None), P(("grp", "loc"), None)),
        check_vma=False,
    )
```

```python
import jax
import jax.numpy as jnp
from jax import lax
from jax.experimental import pallas as pl
from jax.experimental.pallas import tpu as pltpu
from jax.sharding import PartitionSpec as P

STEP = 1000
VMEM = 60 * 1024 * 1024
MESH = pl.DeviceIdType.MESH
F32, BF16, I32 = jnp.float32, jnp.bfloat16, jnp.int32

NY, NXC, NL, CAP = 8, 8, 12, 3
ROWS, WIDTH = 1024, 128
SROWS = 40
LANES = NXC * SROWS
GROUPS = (((0,), 24), ((1, 2), 40), ((3, 4), 40), ((5, 6, 7), 48))
GROUP_OF = (0, 1, 1, 2, 2, 3, 3, 3)
FLAG = 127


def iota(shape, dim):
    return lax.broadcasted_iota(I32, shape, dim)


def onehot(mask):
    return jnp.where(mask, 1.0, 0.0).astype(BF16)


def split(value):
    high = value.astype(BF16)
    low = (value - high.astype(F32)).astype(BF16)
    return jnp.concatenate([high, low], axis=1)


def join(value):
    return value[:, :WIDTH] + value[:, WIDTH:]


def dot(a, b):
    return jnp.dot(a, b, preferred_element_type=F32)


def dot_t(a, b):
    return lax.dot_general(a, b, (((1,), (1,)), ((), ())), preferred_element_type=F32)


def y_distance(chunk):
    hops = (8 - chunk) // 2
    return hops if chunk % 2 else (8 - hops) % 8


def exchange(
    grad_hbm, owner_hbm, slot_hbm, weights_hbm, first_hbm, second_hbm, new_weights, new_first, new_second, over,
    grad, owner, slot, weights, first, second, parts, zsend0, zsend1, zsend2, zsend3,
    zrecv0, zrecv1, zrecv2, zrecv3, zslot_send, zslot_recv, ssend, frecv, wslots, place, acc, count,
    zsem, zrsem, zssem, zsrsem, ssem, frsem, insem,
):
    load = pltpu.make_async_copy(grad_hbm, grad, insem.at[0])
    load.start()
    ids = [
        pltpu.make_async_copy(owner_hbm, owner, insem.at[4]),
        pltpu.make_async_copy(slot_hbm, slot, insem.at[5]),
    ]
    for copy in ids:
        copy.start()
    grp, loc = lax.axis_index("grp"), lax.axis_index("loc")
    my_y, my_xc = grp // NXC, lax.rem(grp, NXC)
    zsend, zrecv = (zsend0, zsend1, zsend2, zsend3), (zrecv0, zrecv1, zrecv2, zrecv3)

    barrier = pltpu.get_barrier_semaphore()
    for step in range(1, NL):
        pl.semaphore_signal(
            barrier, inc=1, device_id=(grp, lax.rem(loc + step, NL)), device_id_type=MESH
        )

    @pl.loop(1, NY * NXC)
    def _(step):
        pl.semaphore_signal(
            barrier, inc=1, device_id=(lax.rem(grp + step, NY * NXC), loc), device_id_type=MESH
        )

    for copy in ids:
        copy.wait()
    own = owner[...]
    group = lax.shift_right_logical(own * 43691, 19)
    index = own - NL * group
    distance = jnp.bitwise_and(lax.shift_right_logical(group, 3) - my_y + NY, NY - 1)
    xc = jnp.bitwise_and(group, NXC - 1)
    hops = jnp.minimum(distance, NY - distance)
    chunk = jnp.maximum(0, 7 - 2 * hops + (distance > 4).astype(I32))

    def rows(tile):
        return jnp.concatenate([tile[b : b + 1, :] for b in range(8)], axis=1)

    group_of = (chunk >= 1).astype(I32) + (chunk >= 3).astype(I32) + (chunk >= 5).astype(I32)
    earlier = iota((128, 128), 0) < iota((128, 128), 1)

    def rank_of(key):
        key_row = rows(key)
        key_col = jnp.concatenate([key] * 16, axis=0).T
        ranks = []
        for ib in range(8):
            mine = key_row[:, ib * 128 : (ib + 1) * 128]
            total = jnp.zeros((128, 128), F32)
            for jb in range(ib + 1):
                same = key_col[:, jb : jb + 1] == mine
                if jb == ib:
                    same = jnp.logical_and(same, earlier)
                total = total + jnp.where(same, 1.0, 0.0)
            ranks.append(jnp.sum(total, axis=0, keepdims=True))
        return jnp.concatenate(ranks, axis=1).astype(I32)

    rank = rank_of(own.astype(F32))
    zrank = rank_of((index * 4 + group_of).astype(F32))
    chunk_row, index_row, xc_row, group_row = rows(chunk), rows(index), rows(xc), rows(group_of)
    room = jnp.full((1, ROWS), GROUPS[0][1], I32)
    for q in range(1, len(GROUPS)):
        room = jnp.where(group_row == q, GROUPS[q][1], room)
    too_many = jnp.max(jnp.where(zrank >= room, 1.0, 0.0), axis=1, keepdims=True)
    code = jnp.where(zrank < room, index_row * room + zrank, -1)

    slot_row = rows(slot[...]) + 1
    line = index_row * NY + chunk_row == iota((NL * NY, ROWS), 0)
    high = lax.shift_right_logical(slot_row, 5).astype(F32)
    low = jnp.bitwise_and(slot_row, 31).astype(F32)
    lines = jnp.concatenate([jnp.where(line, high, 0.0), jnp.where(line, low, 0.0)], axis=0)
    place_lane = onehot(rank * NXC + xc_row == iota((128, ROWS), 0))
    slots = dot_t(lines.astype(BF16), place_lane)
    slots = 32.0 * slots[: NL * NY] + slots[NL * NY :]
    spot = jnp.where(line, jnp.minimum(zrank, 127).astype(F32) + 1.0, 0.0).astype(BF16)
    spot_lane = onehot(rank * NXC + xc_row + 64 == iota((128, ROWS), 0))
    slots = slots + dot_t(spot, spot_lane)
    slots = jnp.where(iota((NL * NY, 128), 1) == FLAG, too_many, slots)
    zslot_send[...] = slots.reshape(NL, NY, 128)

    load.wait()
    parts[...] = split(grad[...])

    def z_compute(q):
        many = NL * GROUPS[q][1]
        here = jnp.where(group_row == q, code, -1)
        pick = onehot(here == iota((many, ROWS), 0))
        out = join(dot(pick, parts[...]))
        zsend[q][...] = out.reshape(NL, GROUPS[q][1], WIDTH)
        zrecv[q][loc] = zsend[q][loc]

    z_compute(0)
    zslot_recv[loc] = zslot_send[loc]
    pl.semaphore_wait(barrier, NL - 1 + NY * NXC - 1)

    z_order = (6, 5, 7, 4, 8, 3, 9, 2, 10, 1, 11)
    for step in z_order:
        to = lax.rem(loc + step, NL)
        pltpu.make_async_remote_copy(
            zslot_send.at[to], zslot_recv.at[loc], zssem, zsrsem,
            device_id=(grp, to), device_id_type=MESH,
        ).start()

    def z_send(q):
        for step in z_order:
            to = lax.rem(loc + step, NL)
            pltpu.make_async_remote_copy(
                zsend[q].at[to], zrecv[q].at[loc], zsem.at[q], zrsem.at[q],
                device_id=(grp, to), device_id_type=MESH,
            ).start()

    def wait(block, sem):
        pltpu.make_async_copy(block, block, sem).wait()

    z_send(0)
    for q in range(1, len(GROUPS)):
        z_compute(q)
        z_send(q)

    tables = [
        pltpu.make_async_copy(weights_hbm, weights, insem.at[1]),
        pltpu.make_async_copy(first_hbm, first, insem.at[2]),
        pltpu.make_async_copy(second_hbm, second, insem.at[3]),
    ]
    for table in tables:
        table.start()

    acc[...] = jnp.zeros_like(acc)
    count[...] = jnp.zeros_like(count)
    over[...] = jnp.zeros_like(over)

    wait(zslot_send.at[pl.ds(0, NL - 1)], zsrsem)
    got = jnp.concatenate([zslot_recv[...].reshape(NL * NY, 128), jnp.zeros((32, 128), F32)], axis=0).T
    high = jnp.floor(got * (1.0 / 32.0))
    low = got - 32.0 * high
    flagged = jnp.sum(got[FLAG : FLAG + 1, :], axis=1, keepdims=True)
    lane = iota((128, 384), 1) - my_xc * SROWS
    line = iota((128, 384), 0)
    def prepare(c):
        total = jnp.zeros((NXC, 384), F32)
        for k in range(CAP):
            part = slice(k * NXC, (k + 1) * NXC)
            both = jnp.concatenate([high[part], low[part]], axis=0).astype(BF16)
            at = onehot(jnp.logical_and(lane == (line // NY) * CAP + k, line % NY == c))
            moved = dot(both, at)
            total = total + 32.0 * moved[:NXC] + moved[NXC:]
        wslots[c] = jnp.where(iota((NXC, 384), 1) == 256 + FLAG, flagged, total)

        spots = jnp.zeros((NXC, 128), F32)
        for k in range(CAP):
            part = slice(64 + k * NXC, 64 + (k + 1) * NXC)
            from_line, to_lane = iota((128, 128), 0), iota((128, 128), 1)
            at = jnp.logical_and(to_lane == (from_line // NY) * CAP + k, from_line % NY == c)
            spots = spots + dot(got[part].astype(BF16), onehot(at))
        spots = jnp.concatenate([spots, jnp.zeros((120, 128), F32)], axis=0).T
        size = GROUPS[GROUP_OF[c]][1]
        column = jnp.concatenate([spots[:SROWS, x : x + 1] for x in range(NXC)], axis=0).astype(I32)
        source = (iota((LANES, 1), 0) % SROWS) // CAP
        column = jnp.where(column > 0, source * size + column - 1, -1)
        place[c, :, : NL * size] = onehot(column == iota((LANES, NL * size), 1))

    def s_stage(c):
        q = GROUP_OF[c]
        many = NL * GROUPS[q][1]
        if c == GROUPS[q][0][0]:
            wait(zsend[q].at[pl.ds(0, NL - 1)], zrsem.at[q])
        moved = join(dot(place[c, :, :many], split(zrecv[q][...].reshape(many, WIDTH))))
        ssend[c] = moved.reshape(NXC, SROWS, WIDTH)
        for x in range(NXC):
            for t in range(3):
                row = NL * CAP + t
                ssend[c, x, row : row + 1, :] = wslots[c, x : x + 1, t * 128 : (t + 1) * 128]

    def s_send(chunks):
        for step in range(NXC):
            to = lax.rem(my_xc + step, NXC)
            for c in chunks:
                away = y_distance(c)
                if away == 0 and step == 0:
                    frecv[c, my_xc] = ssend[c, my_xc]
                    continue
                to_y = lax.rem(my_y + away, NY)
                pltpu.make_async_remote_copy(
                    ssend.at[c, to], frecv.at[c, my_xc], ssem.at[c], frsem.at[c],
                    device_id=(to_y * NXC + to, loc), device_id_type=MESH,
                ).start()

    def f_stage(c):
        many = NXC - 1 if y_distance(c) == 0 else NXC
        wait(ssend.at[c, pl.ds(0, many)], frsem.at[c])
        got = frecv[c]
        line = jnp.sum(got[:, NL * CAP : NL * CAP + 3, :], axis=0)
        line = jnp.concatenate([line[t : t + 1, :] for t in range(3)], axis=1).astype(I32)
        data = split(got.reshape(LANES, WIDTH))
        over[...] += line[:, 256:]

        @pl.loop(0, 4)
        def _(b):
            at = pl.ds(pl.multiple_of(b * 256, 256), 256)
            hit = jnp.where(line == iota((256, 384), 0) + (b * 256 + 1), 1.0, 0.0)
            acc[at, :] += dot(hit[:, :LANES].astype(BF16), data)
            count[at, :] += hit[:, :128] + hit[:, 128:256] + hit[:, 256:]

    def s_group(q):
        for c in GROUPS[q][0]:
            prepare(c)
        for c in GROUPS[q][0]:
            s_stage(c)
        s_send(GROUPS[q][0])

    for q in range(len(GROUPS)):
        s_group(q)
    for c in (0, 1, 2, 3, 4, 7, 5):
        f_stage(c)
    for table in tables:
        table.wait()
    f_stage(6)

    for b in range(4):
        at = pl.ds(b * 256, 256)
        summed = join(acc[at, :])
        active = dot(count[at, :].astype(BF16), jnp.ones((128, WIDTH), BF16)) > 0.5
        old_first, old_second, old_weights = first[at, :], second[at, :], weights[at, :]
        first_next = 0.9 * old_first + 0.1 * summed
        second_next = 0.99 * old_second + 0.01 * summed * summed
        first_hat = first_next / (1.0 - 0.9**STEP)
        second_hat = second_next / (1.0 - 0.99**STEP)
        weights_next = old_weights - 0.5 * first_hat / (jnp.sqrt(second_hat) + 1e-08)
        new_first[at, :] = jnp.where(active, first_next, old_first)
        new_second[at, :] = jnp.where(active, second_next, old_second)
        new_weights[at, :] = jnp.where(active, weights_next, old_weights)

    wait(zslot_send.at[pl.ds(0, NL - 1)], zssem)
    for q in range(len(GROUPS)):
        wait(zsend[q].at[pl.ds(0, NL - 1)], zsem.at[q])
    for c in range(NY):
        many = NXC - 1 if y_distance(c) == 0 else NXC
        wait(ssend.at[c, pl.ds(0, many)], ssem.at[c])


def store(weights, first, second, weights_hbm, first_hbm, second_hbm, sems):
    pairs = ((weights, weights_hbm), (first, first_hbm), (second, second_hbm))
    copies = [pltpu.make_async_copy(a, b, sems.at[i]) for i, (a, b) in enumerate(pairs)]
    for copy in copies:
        copy.start()
    for copy in copies:
        copy.wait()


def padded(grad_rows, row_owner, row_slot, weights, first_moment, second_moment):
    group_count = lax.axis_size("grp")
    local_count = lax.axis_size("loc")
    devices_all = group_count * local_count
    rows, width = grad_rows.shape
    shard = weights.shape[0]
    capacity = max(2, (2 * rows + devices_all - 1) // devices_all)
    owner = row_owner[:, 0]
    same_owner = owner[:, None] == owner[None, :]
    before = lax.broadcasted_iota(jnp.int32, (rows, rows), 1) < lax.broadcasted_iota(
        jnp.int32, (rows, rows), 0
    )
    rank = jnp.sum(jnp.logical_and(same_owner, before).astype(jnp.int32), axis=1)
    position = owner * capacity + rank
    send_grads = jnp.zeros((devices_all * capacity, width), jnp.float32).at[position].set(grad_rows)
    send_slots = jnp.full((devices_all * capacity,), -1, jnp.int32).at[position].set(row_slot)
    send_grads = send_grads.reshape(group_count, local_count, capacity, width)
    send_slots = send_slots.reshape(group_count, local_count, capacity)
    middle = (
        lax.all_to_all(send_grads, "loc", split_axis=1, concat_axis=1, tiled=True),
        lax.all_to_all(send_slots, "loc", split_axis=1, concat_axis=1, tiled=True),
    )
    arrived = (
        lax.all_to_all(middle[0], "grp", split_axis=0, concat_axis=0, tiled=True),
        lax.all_to_all(middle[1], "grp", split_axis=0, concat_axis=0, tiled=True),
    )
    got_grads = arrived[0].reshape(devices_all * capacity, width)
    got_slots = arrived[1].reshape(devices_all * capacity)
    table_index = lax.broadcasted_iota(jnp.int32, (shard, devices_all * capacity), 0)
    selector = (table_index == got_slots[None, :]).astype(jnp.float32)
    summed = jnp.dot(
        selector, got_grads, precision=lax.Precision.HIGHEST, preferred_element_type=jnp.float32
    )
    touched = jnp.sum(selector, axis=1)
    active = (touched > 0.5)[:, None]
    first_next = 0.9 * first_moment + 0.1 * summed
    second_next = 0.99 * second_moment + 0.01 * summed * summed
    first_hat = first_next / (1.0 - 0.9**STEP)
    second_hat = second_next / (1.0 - 0.99**STEP)
    weights_next = weights - 0.5 * first_hat / (jnp.sqrt(second_hat) + 1e-08)
    new_first = jnp.where(active, first_next, first_moment)
    new_second = jnp.where(active, second_next, second_moment)
    new_weights = jnp.where(active, weights_next, weights)
    return (new_weights, new_first, new_second)


def on_device(grad_rows, row_owner, row_slot, weights, first_moment, second_moment):
    vmem = pl.BlockSpec(memory_space=pltpu.VMEM)
    dma = pltpu.SemaphoreType.DMA
    hbm = pl.BlockSpec(memory_space=pltpu.HBM)
    out = jax.ShapeDtypeStruct((ROWS, WIDTH), F32)
    *results, over = pl.pallas_call(
        exchange,
        out_shape=(out, out, out, jax.ShapeDtypeStruct((1, 128), I32)),
        in_specs=[hbm] * 6,
        out_specs=(vmem, vmem, vmem, vmem),
        scratch_shapes=[
            pltpu.VMEM((ROWS, WIDTH), F32),
            pltpu.VMEM((8, 128), I32),
            pltpu.VMEM((8, 128), I32),
            pltpu.VMEM((ROWS, WIDTH), F32),
            pltpu.VMEM((ROWS, WIDTH), F32),
            pltpu.VMEM((ROWS, WIDTH), F32),
            pltpu.VMEM((ROWS, 2 * WIDTH), BF16),
            *[pltpu.VMEM((NL, room, WIDTH), F32) for _, room in GROUPS],
            *[pltpu.VMEM((NL, room, WIDTH), F32) for _, room in GROUPS],
            pltpu.VMEM((NL, NY, 128), F32),
            pltpu.VMEM((NL, NY, 128), F32),
            pltpu.VMEM((NY, NXC, SROWS, WIDTH), F32),
            pltpu.VMEM((NY, NXC, SROWS, WIDTH), F32),
            pltpu.VMEM((NY, NXC, 384), F32),
            pltpu.VMEM((NY, LANES, 640), BF16),
            pltpu.VMEM((ROWS, 2 * WIDTH), F32),
            pltpu.VMEM((ROWS, 128), F32),
            dma((len(GROUPS),)),
            dma((len(GROUPS),)),
            dma,
            dma,
            dma((NY,)),
            dma((NY,)),
            dma((6,)),
        ],
        compiler_params=pltpu.CompilerParams(
            collective_id=0, has_side_effects=True, vmem_limit_bytes=VMEM
        ),
        name="exchange",
    )(
        grad_rows, row_owner.reshape(8, 128), row_slot.reshape(8, 128),
        weights, first_moment, second_moment,
    )
    def packed():
        return pl.pallas_call(
            store,
            out_shape=(out, out, out),
            in_specs=[vmem] * 3,
            out_specs=(hbm, hbm, hbm),
            scratch_shapes=[dma((3,))],
            compiler_params=pltpu.CompilerParams(vmem_limit_bytes=VMEM),
            name="store",
        )(*results)

    def full():
        return tuple(padded(grad_rows, row_owner, row_slot, weights, first_moment, second_moment))

    return lax.cond(over[0, FLAG] > 0, full, packed)


def solution(mesh):
    placed = (
        P(("grp", "loc"), None),
        P(("grp", "loc"), None),
        P(("grp", "loc")),
        P(("grp", "loc"), None),
        P(("grp", "loc"), None),
        P(("grp", "loc"), None),
    )
    return jax.shard_map(
        on_device,
        mesh=mesh,
        in_specs=placed,
        out_specs=(P(("grp", "loc"), None), P(("grp", "loc"), None), P(("grp", "loc"), None)),
        check_vma=False,
    )
```

```python
import jax
import jax.numpy as jnp
from jax import lax
from jax.experimental import pallas as pl
from jax.experimental.pallas import tpu as pltpu
from jax.sharding import PartitionSpec as P

STEP = 1000
VMEM = 60 * 1024 * 1024
MESH = pl.DeviceIdType.MESH
F32, BF16, I32 = jnp.float32, jnp.bfloat16, jnp.int32

NY, NXC, NL, CAP = 8, 8, 12, 3
ROWS, WIDTH = 1024, 128
SROWS = 40
LANES = NXC * SROWS
GROUPS = (((0,), 24), ((1, 2), 40), ((3, 4), 40), ((5, 6, 7), 48))
GROUP_OF = (0, 1, 1, 2, 2, 3, 3, 3)
FLAG = 127


def iota(shape, dim):
    return lax.broadcasted_iota(I32, shape, dim)


def onehot(mask):
    return jnp.where(mask, 1.0, 0.0).astype(BF16)


def split(value):
    high = value.astype(BF16)
    low = (value - high.astype(F32)).astype(BF16)
    return jnp.concatenate([high, low], axis=1)


def join(value):
    return value[:, :WIDTH] + value[:, WIDTH:]


def dot(a, b):
    return jnp.dot(a, b, preferred_element_type=F32)


def dot_t(a, b):
    return lax.dot_general(a, b, (((1,), (1,)), ((), ())), preferred_element_type=F32)


def y_distance(chunk):
    hops = (8 - chunk) // 2
    return hops if chunk % 2 else (8 - hops) % 8


def exchange(
    grad_hbm, owner_hbm, slot_hbm, weights_hbm, first_hbm, second_hbm, new_weights, new_first, new_second, over,
    grad, owner, slot, weights, first, second, parts, zsend0, zsend1, zsend2, zsend3,
    zrecv0, zrecv1, zrecv2, zrecv3, zslot_send, zslot_recv, ssend, frecv, wslots, place, acc, count,
    zsem, zrsem, zssem, zsrsem, ssem, frsem, insem,
):
    load = pltpu.make_async_copy(grad_hbm, grad, insem.at[0])
    load.start()
    ids = [
        pltpu.make_async_copy(owner_hbm, owner, insem.at[4]),
        pltpu.make_async_copy(slot_hbm, slot, insem.at[5]),
    ]
    for copy in ids:
        copy.start()
    grp, loc = lax.axis_index("grp"), lax.axis_index("loc")
    my_y, my_xc = grp // NXC, lax.rem(grp, NXC)
    zsend, zrecv = (zsend0, zsend1, zsend2, zsend3), (zrecv0, zrecv1, zrecv2, zrecv3)

    barrier = pltpu.get_barrier_semaphore()
    for step in range(1, NL):
        pl.semaphore_signal(
            barrier, inc=1, device_id=(grp, lax.rem(loc + step, NL)), device_id_type=MESH
        )

    @pl.loop(1, NY * NXC)
    def _(step):
        pl.semaphore_signal(
            barrier, inc=1, device_id=(lax.rem(grp + step, NY * NXC), loc), device_id_type=MESH
        )

    for copy in ids:
        copy.wait()
    own = owner[...]
    group = lax.shift_right_logical(own * 43691, 19)
    index = own - NL * group
    distance = jnp.bitwise_and(lax.shift_right_logical(group, 3) - my_y + NY, NY - 1)
    xc = jnp.bitwise_and(group, NXC - 1)
    hops = jnp.minimum(distance, NY - distance)
    chunk = jnp.maximum(0, 7 - 2 * hops + (distance > 4).astype(I32))

    def rows(tile):
        return jnp.concatenate([tile[b : b + 1, :] for b in range(8)], axis=1)

    group_of = (chunk >= 1).astype(I32) + (chunk >= 3).astype(I32) + (chunk >= 5).astype(I32)
    earlier = iota((128, 128), 0) < iota((128, 128), 1)

    def rank_of(key):
        key_row = rows(key)
        key_col = jnp.concatenate([key] * 16, axis=0).T
        ranks = []
        for ib in range(8):
            mine = key_row[:, ib * 128 : (ib + 1) * 128]
            total = jnp.zeros((128, 128), F32)
            for jb in range(ib + 1):
                same = key_col[:, jb : jb + 1] == mine
                if jb == ib:
                    same = jnp.logical_and(same, earlier)
                total = total + jnp.where(same, 1.0, 0.0)
            ranks.append(jnp.sum(total, axis=0, keepdims=True))
        return jnp.concatenate(ranks, axis=1).astype(I32)

    rank = rank_of(own.astype(F32))
    zrank = rank_of((index * 4 + group_of).astype(F32))
    chunk_row, index_row, xc_row, group_row = rows(chunk), rows(index), rows(xc), rows(group_of)
    room = jnp.full((1, ROWS), GROUPS[0][1], I32)
    for q in range(1, len(GROUPS)):
        room = jnp.where(group_row == q, GROUPS[q][1], room)
    too_many = jnp.max(jnp.where(zrank >= room, 1.0, 0.0), axis=1, keepdims=True)
    code = jnp.where(zrank < room, index_row * room + zrank, -1)

    slot_row = rows(slot[...]) + 1
    line = index_row * NY + chunk_row == iota((NL * NY, ROWS), 0)
    high = lax.shift_right_logical(slot_row, 5).astype(F32)
    low = jnp.bitwise_and(slot_row, 31).astype(F32)
    lines = jnp.concatenate([jnp.where(line, high, 0.0), jnp.where(line, low, 0.0)], axis=0)
    place_lane = onehot(rank * NXC + xc_row == iota((128, ROWS), 0))
    slots = dot_t(lines.astype(BF16), place_lane)
    slots = 32.0 * slots[: NL * NY] + slots[NL * NY :]
    spot = jnp.where(line, jnp.minimum(zrank, 127).astype(F32) + 1.0, 0.0).astype(BF16)
    spot_lane = onehot(rank * NXC + xc_row + 64 == iota((128, ROWS), 0))
    slots = slots + dot_t(spot, spot_lane)
    slots = jnp.where(iota((NL * NY, 128), 1) == FLAG, too_many, slots)
    zslot_send[...] = slots.reshape(NL, NY, 128)

    load.wait()
    parts[...] = split(grad[...])

    def z_compute(q):
        many = NL * GROUPS[q][1]
        here = jnp.where(group_row == q, code, -1)
        pick = onehot(here == iota((many, ROWS), 0))
        out = join(dot(pick, parts[...]))
        zsend[q][...] = out.reshape(NL, GROUPS[q][1], WIDTH)
        zrecv[q][loc] = zsend[q][loc]

    z_compute(0)
    zslot_recv[loc] = zslot_send[loc]
    pl.semaphore_wait(barrier, NL - 1 + NY * NXC - 1)

    z_order = (6, 5, 7, 4, 8, 3, 9, 2, 10, 1, 11)
    for step in z_order:
        to = lax.rem(loc + step, NL)
        pltpu.make_async_remote_copy(
            zslot_send.at[to], zslot_recv.at[loc], zssem, zsrsem,
            device_id=(grp, to), device_id_type=MESH,
        ).start()

    def z_send(q):
        for step in z_order:
            to = lax.rem(loc + step, NL)
            pltpu.make_async_remote_copy(
                zsend[q].at[to], zrecv[q].at[loc], zsem.at[q], zrsem.at[q],
                device_id=(grp, to), device_id_type=MESH,
            ).start()

    def wait(block, sem):
        pltpu.make_async_copy(block, block, sem).wait()

    z_send(0)
    for q in range(1, len(GROUPS)):
        z_compute(q)
        z_send(q)

    tables = [
        pltpu.make_async_copy(weights_hbm, weights, insem.at[1]),
        pltpu.make_async_copy(first_hbm, first, insem.at[2]),
        pltpu.make_async_copy(second_hbm, second, insem.at[3]),
    ]
    for table in tables:
        table.start()

    acc[...] = jnp.zeros_like(acc)
    count[...] = jnp.zeros_like(count)
    over[...] = jnp.zeros_like(over)

    wait(zslot_send.at[pl.ds(0, NL - 1)], zsrsem)
    got = jnp.concatenate([zslot_recv[...].reshape(NL * NY, 128), jnp.zeros((32, 128), F32)], axis=0).T
    high = jnp.floor(got * (1.0 / 32.0))
    low = got - 32.0 * high
    flagged = jnp.sum(got[FLAG : FLAG + 1, :], axis=1, keepdims=True)
    lane = iota((128, 384), 1) - my_xc * SROWS
    line = iota((128, 384), 0)
    def prepare(c):
        total = jnp.zeros((NXC, 384), F32)
        for k in range(CAP):
            part = slice(k * NXC, (k + 1) * NXC)
            both = jnp.concatenate([high[part], low[part]], axis=0).astype(BF16)
            at = onehot(jnp.logical_and(lane == (line // NY) * CAP + k, line % NY == c))
            moved = dot(both, at)
            total = total + 32.0 * moved[:NXC] + moved[NXC:]
        wslots[c] = jnp.where(iota((NXC, 384), 1) == 256 + FLAG, flagged, total)

        spots = jnp.zeros((NXC, 128), F32)
        for k in range(CAP):
            part = slice(64 + k * NXC, 64 + (k + 1) * NXC)
            from_line, to_lane = iota((128, 128), 0), iota((128, 128), 1)
            at = jnp.logical_and(to_lane == (from_line // NY) * CAP + k, from_line % NY == c)
            spots = spots + dot(got[part].astype(BF16), onehot(at))
        spots = jnp.concatenate([spots, jnp.zeros((120, 128), F32)], axis=0).T
        size = GROUPS[GROUP_OF[c]][1]
        column = jnp.concatenate([spots[:SROWS, x : x + 1] for x in range(NXC)], axis=0).astype(I32)
        source = (iota((LANES, 1), 0) % SROWS) // CAP
        column = jnp.where(column > 0, source * size + column - 1, -1)
        place[c, :, : NL * size] = onehot(column == iota((LANES, NL * size), 1))

    def s_stage(c):
        q = GROUP_OF[c]
        many = NL * GROUPS[q][1]
        if c == GROUPS[q][0][0]:
            wait(zsend[q].at[pl.ds(0, NL - 1)], zrsem.at[q])
        moved = join(dot(place[c, :, :many], split(zrecv[q][...].reshape(many, WIDTH))))
        ssend[c] = moved.reshape(NXC, SROWS, WIDTH)
        for x in range(NXC):
            for t in range(3):
                row = NL * CAP + t
                ssend[c, x, row : row + 1, :] = wslots[c, x : x + 1, t * 128 : (t + 1) * 128]

    def s_send(chunks):
        for step in range(NXC):
            to = lax.rem(my_xc + step, NXC)
            for c in chunks:
                away = y_distance(c)
                if away == 0 and step == 0:
                    frecv[c, my_xc] = ssend[c, my_xc]
                    continue
                to_y = lax.rem(my_y + away, NY)
                pltpu.make_async_remote_copy(
                    ssend.at[c, to], frecv.at[c, my_xc], ssem.at[c], frsem.at[c],
                    device_id=(to_y * NXC + to, loc), device_id_type=MESH,
                ).start()

    def f_stage(c):
        many = NXC - 1 if y_distance(c) == 0 else NXC
        wait(ssend.at[c, pl.ds(0, many)], frsem.at[c])
        got = frecv[c]
        line = jnp.sum(got[:, NL * CAP : NL * CAP + 3, :], axis=0)
        line = jnp.concatenate([line[t : t + 1, :] for t in range(3)], axis=1).astype(I32)
        data = split(got.reshape(LANES, WIDTH))
        over[...] += jnp.where(iota((1, 128), 1) == FLAG, line[:, 256:], 0)

        @pl.loop(0, 4)
        def _(b):
            at = pl.ds(pl.multiple_of(b * 256, 256), 256)
            hit = jnp.where(line == iota((256, 384), 0) + (b * 256 + 1), 1.0, 0.0)
            acc[at, :] += dot(hit[:, :LANES].astype(BF16), data)
            count[at, :] += hit[:, :128] + hit[:, 128:256] + hit[:, 256:]

    def s_group(q):
        for c in GROUPS[q][0]:
            prepare(c)
        for c in GROUPS[q][0]:
            s_stage(c)
        s_send(GROUPS[q][0])

    for q in range(len(GROUPS)):
        s_group(q)
    for c in (0, 1, 2, 3, 4, 7, 5):
        f_stage(c)
    for table in tables:
        table.wait()
    f_stage(6)

    for b in range(4):
        at = pl.ds(b * 256, 256)
        summed = join(acc[at, :])
        active = dot(count[at, :].astype(BF16), jnp.ones((128, WIDTH), BF16)) > 0.5
        old_first, old_second, old_weights = first[at, :], second[at, :], weights[at, :]
        first_next = 0.9 * old_first + 0.1 * summed
        second_next = 0.99 * old_second + 0.01 * summed * summed
        first_hat = first_next / (1.0 - 0.9**STEP)
        second_hat = second_next / (1.0 - 0.99**STEP)
        weights_next = old_weights - 0.5 * first_hat / (jnp.sqrt(second_hat) + 1e-08)
        new_first[at, :] = jnp.where(active, first_next, old_first)
        new_second[at, :] = jnp.where(active, second_next, old_second)
        new_weights[at, :] = jnp.where(active, weights_next, old_weights)

    wait(zslot_send.at[pl.ds(0, NL - 1)], zssem)
    for q in range(len(GROUPS)):
        wait(zsend[q].at[pl.ds(0, NL - 1)], zsem.at[q])
    for c in range(NY):
        many = NXC - 1 if y_distance(c) == 0 else NXC
        wait(ssend.at[c, pl.ds(0, many)], ssem.at[c])


def store(weights, first, second, weights_hbm, first_hbm, second_hbm, sems):
    pairs = ((weights, weights_hbm), (first, first_hbm), (second, second_hbm))
    copies = [pltpu.make_async_copy(a, b, sems.at[i]) for i, (a, b) in enumerate(pairs)]
    for copy in copies:
        copy.start()
    for copy in copies:
        copy.wait()


def padded(grad_rows, row_owner, row_slot, weights, first_moment, second_moment):
    group_count = lax.axis_size("grp")
    local_count = lax.axis_size("loc")
    devices_all = group_count * local_count
    rows, width = grad_rows.shape
    shard = weights.shape[0]
    capacity = max(2, (2 * rows + devices_all - 1) // devices_all)
    owner = row_owner[:, 0]
    same_owner = owner[:, None] == owner[None, :]
    before = lax.broadcasted_iota(jnp.int32, (rows, rows), 1) < lax.broadcasted_iota(
        jnp.int32, (rows, rows), 0
    )
    rank = jnp.sum(jnp.logical_and(same_owner, before).astype(jnp.int32), axis=1)
    position = owner * capacity + rank
    send_grads = jnp.zeros((devices_all * capacity, width), jnp.float32).at[position].set(grad_rows)
    send_slots = jnp.full((devices_all * capacity,), -1, jnp.int32).at[position].set(row_slot)
    send_grads = send_grads.reshape(group_count, local_count, capacity, width)
    send_slots = send_slots.reshape(group_count, local_count, capacity)
    middle = (
        lax.all_to_all(send_grads, "loc", split_axis=1, concat_axis=1, tiled=True),
        lax.all_to_all(send_slots, "loc", split_axis=1, concat_axis=1, tiled=True),
    )
    arrived = (
        lax.all_to_all(middle[0], "grp", split_axis=0, concat_axis=0, tiled=True),
        lax.all_to_all(middle[1], "grp", split_axis=0, concat_axis=0, tiled=True),
    )
    got_grads = arrived[0].reshape(devices_all * capacity, width)
    got_slots = arrived[1].reshape(devices_all * capacity)
    table_index = lax.broadcasted_iota(jnp.int32, (shard, devices_all * capacity), 0)
    selector = (table_index == got_slots[None, :]).astype(jnp.float32)
    summed = jnp.dot(
        selector, got_grads, precision=lax.Precision.HIGHEST, preferred_element_type=jnp.float32
    )
    touched = jnp.sum(selector, axis=1)
    active = (touched > 0.5)[:, None]
    first_next = 0.9 * first_moment + 0.1 * summed
    second_next = 0.99 * second_moment + 0.01 * summed * summed
    first_hat = first_next / (1.0 - 0.9**STEP)
    second_hat = second_next / (1.0 - 0.99**STEP)
    weights_next = weights - 0.5 * first_hat / (jnp.sqrt(second_hat) + 1e-08)
    new_first = jnp.where(active, first_next, first_moment)
    new_second = jnp.where(active, second_next, second_moment)
    new_weights = jnp.where(active, weights_next, weights)
    return (new_weights, new_first, new_second)


def on_device(grad_rows, row_owner, row_slot, weights, first_moment, second_moment):
    vmem = pl.BlockSpec(memory_space=pltpu.VMEM)
    dma = pltpu.SemaphoreType.DMA
    hbm = pl.BlockSpec(memory_space=pltpu.HBM)
    out = jax.ShapeDtypeStruct((ROWS, WIDTH), F32)
    *results, over = pl.pallas_call(
        exchange,
        out_shape=(out, out, out, jax.ShapeDtypeStruct((1, 128), I32)),
        in_specs=[hbm] * 6,
        out_specs=(vmem, vmem, vmem, vmem),
        scratch_shapes=[
            pltpu.VMEM((ROWS, WIDTH), F32),
            pltpu.VMEM((8, 128), I32),
            pltpu.VMEM((8, 128), I32),
            pltpu.VMEM((ROWS, WIDTH), F32),
            pltpu.VMEM((ROWS, WIDTH), F32),
            pltpu.VMEM((ROWS, WIDTH), F32),
            pltpu.VMEM((ROWS, 2 * WIDTH), BF16),
            *[pltpu.VMEM((NL, room, WIDTH), F32) for _, room in GROUPS],
            *[pltpu.VMEM((NL, room, WIDTH), F32) for _, room in GROUPS],
            pltpu.VMEM((NL, NY, 128), F32),
            pltpu.VMEM((NL, NY, 128), F32),
            pltpu.VMEM((NY, NXC, SROWS, WIDTH), F32),
            pltpu.VMEM((NY, NXC, SROWS, WIDTH), F32),
            pltpu.VMEM((NY, NXC, 384), F32),
            pltpu.VMEM((NY, LANES, 640), BF16),
            pltpu.VMEM((ROWS, 2 * WIDTH), F32),
            pltpu.VMEM((ROWS, 128), F32),
            dma((len(GROUPS),)),
            dma((len(GROUPS),)),
            dma,
            dma,
            dma((NY,)),
            dma((NY,)),
            dma((6,)),
        ],
        compiler_params=pltpu.CompilerParams(
            collective_id=0, has_side_effects=True, vmem_limit_bytes=VMEM
        ),
        name="exchange",
    )(
        grad_rows, row_owner.reshape(8, 128), row_slot.reshape(8, 128),
        weights, first_moment, second_moment,
    )
    def packed():
        return pl.pallas_call(
            store,
            out_shape=(out, out, out),
            in_specs=[vmem] * 3,
            out_specs=(hbm, hbm, hbm),
            scratch_shapes=[dma((3,))],
            compiler_params=pltpu.CompilerParams(vmem_limit_bytes=VMEM),
            name="store",
        )(*results)

    def full():
        return tuple(padded(grad_rows, row_owner, row_slot, weights, first_moment, second_moment))

    return lax.cond(jnp.max(over) > 0, full, packed)


def solution(mesh):
    placed = (
        P(("grp", "loc"), None),
        P(("grp", "loc"), None),
        P(("grp", "loc")),
        P(("grp", "loc"), None),
        P(("grp", "loc"), None),
        P(("grp", "loc"), None),
    )
    return jax.shard_map(
        on_device,
        mesh=mesh,
        in_specs=placed,
        out_specs=(P(("grp", "loc"), None), P(("grp", "loc"), None), P(("grp", "loc"), None)),
        check_vma=False,
    )
```
